256 devices in a mesh: dp: 32 (over z_lo, y, core), feat: 8 (over z_hi, x).
Axes of the slice: x: 4, y: 4, z: 8 (z_hi: 2, z_lo: 4; z = z_hi * 4 + z_lo), core: 2. Of those that a mesh axis runs over, the one named last changes fastest.
Arguments:
- table: bfloat16 [4096, 3584], P('dp', 'feat'), may hold values from -64 to 64
- text: bfloat16 [4096, 3584], P('dp', 'feat'), may hold values from -64 to 64
- table_proj: bfloat16 [3584, 4096], P(None, 'feat'), may hold values from -1 to 1
- text_proj: bfloat16 [3584, 4096], P(None, 'feat'), may hold values from -1 to 1
Outputs:
- grad_table: float32 [4096, 3584], P('dp', 'feat')
- grad_text: float32 [4096, 3584], P('dp', 'feat')
- loss_mean: float32 [1], replicated
The draws below stay inside these ranges and needn't reach their ends.
All inputs are finite; a program needn't handle non-finite values.
Results may differ from the reference program's by a relative error of at most 0.0044.
Values may be sent and summed in bfloat16 or wider, within the bound.
A program may use at most 64 MiB of HBM per device.

```python
import jax
import jax.numpy as jnp
from jax import lax

E = 3584
F = 4096
PAIRS = 4096


def embed_shared(key):
    key_row, key_col, key_base = jax.random.split(jax.random.fold_in(key, 5), 3)
    position = jnp.arange(PAIRS).astype(jnp.float32)[:, None] / PAIRS
    rising = jnp.exp(jnp.log(3.0) * position)
    row_scale = 0.3 * rising * jnp.exp(jax.random.uniform(key_row, (PAIRS, 1), jnp.float32, -1.15, 1.15))
    col_scale = jnp.exp(jax.random.uniform(key_col, (1, E), jnp.float32, -0.7, 0.7))
    scale = row_scale * col_scale
    return (scale, key_base)


def embed_noise(key_base):
    return jnp.clip(jax.random.normal(key_base, (PAIRS, E), jnp.float32), -4.0, 4.0)


def embed_draw(key, own_const):
    scale, key_base = embed_shared(key)
    shared = embed_noise(key_base)
    own_key = jax.random.fold_in(key, own_const)
    own_base = jax.random.fold_in(own_key, 0)
    own = embed_noise(own_base)
    return (scale * (0.8 * shared + 0.6 * own)).astype(jnp.bfloat16)


def draw_table(key, part):
    return embed_draw(key, 11)


def draw_text(key, part):
    return embed_draw(key, 23)


def proj_shared(key):
    base = jnp.clip(jax.random.normal(jax.random.fold_in(key, 7), (E, F), jnp.float32), -4.0, 4.0)
    return base * (1.0 / jnp.sqrt(jnp.float32(E)))


def draw_table_proj(key, part):
    return proj_shared(key).astype(jnp.bfloat16)


def draw_text_proj(key, part):
    shared = proj_shared(key)
    key = jax.random.fold_in(key, 31)
    key_noise, key_angle = jax.random.split(key, 2)
    noise = jnp.clip(jax.random.normal(key_noise, (E, F), jnp.float32), -4.0, 4.0) * (1.0 / jnp.sqrt(jnp.float32(E)))
    place = (jnp.arange(F).astype(jnp.float32) + 0.5) / F
    angle = 1.45 * place + jax.random.uniform(key_angle, (F,), jnp.float32, -0.05, 0.05)
    angle = jnp.clip(angle, 0.0, 1.5)
    return (jnp.cos(angle)[None, :] * shared + jnp.sin(angle)[None, :] * noise).astype(jnp.bfloat16)


def setup_inputs(seed: int = 0) -> dict:
    arg_keys = jax.random.split(jax.random.key(seed), 5)
    table = draw_table(jax.random.fold_in(arg_keys[4], 71), 0)
    text = draw_text(jax.random.fold_in(arg_keys[4], 71), 0)
    table_proj = draw_table_proj(jax.random.fold_in(arg_keys[4], 71), 0)
    text_proj = draw_text_proj(jax.random.fold_in(arg_keys[4], 71), 0)
    return {"table": table, "text": text, "table_proj": table_proj, "text_proj": text_proj}


OFF_WEIGHT = 0.1
EPS = 1e-05

def normalize(proj):
    center = lax.optimization_barrier(jnp.mean(proj, axis=0))
    spread = lax.optimization_barrier(jnp.mean(proj * proj, axis=0)) - center * center
    inverse = lax.rsqrt(spread + EPS)
    return ((proj - center) * inverse, inverse)

def backward(grad, normed, inverse):
    shift = lax.optimization_barrier(jnp.mean(grad, axis=0))
    tilt = lax.optimization_barrier(jnp.mean(grad * normed, axis=0))
    return (inverse * (grad - shift - normed * tilt)).astype(jnp.bfloat16)

def reference(table, text, table_proj, text_proj):
    z_table = jnp.dot(table, table_proj, preferred_element_type=jnp.float32)
    z_text = jnp.dot(text, text_proj, preferred_element_type=jnp.float32)
    normed_table, inverse_table = normalize(z_table)
    normed_text, inverse_text = normalize(z_text)
    half_table = normed_table.astype(jnp.bfloat16)
    half_text = normed_text.astype(jnp.bfloat16)
    corr = lax.dot_general(half_table, half_text, (((0,), (0,)), ((), ())), preferred_element_type=jnp.float32) / PAIRS
    row_ids = lax.broadcasted_iota(jnp.int32, (F, F), 0)
    col_ids = lax.broadcasted_iota(jnp.int32, (F, F), 1)
    on_diag = row_ids == col_ids
    terms = jnp.where(on_diag, (1.0 - corr) * (1.0 - corr), OFF_WEIGHT * corr * corr)
    loss_mean = (jnp.sum(terms) / F).reshape(1)
    kernel = jnp.where(on_diag, corr - 1.0, OFF_WEIGHT * corr).astype(jnp.bfloat16)
    d_table = lax.dot_general(half_text, kernel, (((1,), (1,)), ((), ())), preferred_element_type=jnp.float32)
    d_text = jnp.dot(half_table, kernel, preferred_element_type=jnp.float32)
    back_table = backward(d_table, normed_table, inverse_table)
    back_text = backward(d_text, normed_text, inverse_text)
    grad_table = lax.dot_general(back_table, table_proj, (((1,), (1,)), ((), ())), preferred_element_type=jnp.float32)
    grad_text = lax.dot_general(back_text, text_proj, (((1,), (1,)), ((), ())), preferred_element_type=jnp.float32)
    return (grad_table, grad_text, loss_mean)
```

```python
import jax
import jax.numpy as jnp
from jax import lax
from jax.experimental import pallas as pl
from jax.experimental.pallas import tpu as pltpu
from jax.sharding import PartitionSpec as P

OFF_WEIGHT = 0.1
EPS = 1e-05
MESH = pl.DeviceIdType.MESH
BF16, F32 = jnp.bfloat16, jnp.float32
NUM_DP, NUM_FEAT = 32, 8

SLOTS = {}


def _slots(name, count):
    SLOTS[name] = sum(n for _, n in SLOTS.values()), count


for _name, _count in (
    ("emb_z", 1), ("emb_x", 3), ("emb_zx", 3),
    ("st1_a", 7), ("st1_b", 3),
    ("txt_z", 1), ("txt_x", 3), ("txt_zx", 3), ("txt_a2a", 8),
    ("tab_l", 1), ("tab_y", 3), ("tab_ly", 3),
    ("corr_c", 1), ("corr_h", 1), ("ker_c", 1),
    ("dx_a2a", 7), ("dx_x", 8), ("dx_z", 1),
    ("dt_y", 3), ("dt_l", 1),
    ("st2_a", 7), ("st2_b", 3),
    ("gr_far", 3), ("gr_near", 3), ("gr_z", 1),
    ("loss_x", 3), ("loss_z", 1),
):
    _slots(_name, _count)
NUM_SLOTS = sum(n for _, n in SLOTS.values())


def slot(name, i=0):
    return SLOTS[name][0] + i


def matmul(a, b, dims):
    return lax.dot_general(a, b, ((dims[:1], dims[1:]), ((), ())), preferred_element_type=F32)


def kernel(
    table, text, tproj, xproj,
    grad_table, grad_text, loss_out,
    pt, px, emb, z, st_a, st_b, half_full, tab_g, txt_g,
    part, part_c, part_h, part_hr, ker,
    dxp, dx, dx_r, dx_far, dx_zr, dtp, dt_r, dt_far, dt_lr,
    gp, gr, g_own, g_far, g_zr, ls_x, ls_z,
    ssem, rsem, lsem,
):
    rows, width = table.shape
    feats = tproj.shape[1]
    pairs = rows * NUM_DP
    half = feats // 2
    dp, ft = lax.axis_index("dp"), lax.axis_index("feat")
    zl, y, c = dp // 8, (dp // 2) % 4, dp % 2
    h, l = zl // 2, zl % 2
    zh, x = ft // 4, ft % 4

    def device(zl_=zl, y_=y, c_=c, zh_=zh, x_=x):
        return {"dp": (zl_ * 4 + y_) * 2 + c_, "feat": zh_ * 4 + x_}

    z_peer = device(zh_=1 - zh)
    c_peer = device(c_=1 - c)
    l_peer = device(zl_=h * 2 + 1 - l)
    h_peer = device(zl_=(1 - h) * 2 + l)

    def x_peer(i):
        return device(x_=(x + i) % 4)

    def y_peer(i):
        return device(y_=(y + i) % 4)

    yc = [(dy, dc) for dy in range(4) for dc in range(2) if dy or dc]
    yl = [(dy, dl) for dy in range(4) for dl in range(2) if dy or dl]

    def yl_peer(dy, dl):
        return device(y_=(y + dy) % 4, zl_=h * 2 + (l + dl) % 2)

    started = []

    def send(src, dst, s, to, r=None):
        copy = pltpu.make_async_remote_copy(
            src_ref=src, dst_ref=dst, send_sem=ssem.at[s], recv_sem=rsem.at[s if r is None else r],
            device_id=to, device_id_type=MESH,
        )
        copy.start()
        return copy

    def post(src, dst, s, to):
        copy = send(src, dst, s, to)
        started.append(copy)
        return copy

    load_t = pltpu.make_async_copy(tproj, pt, lsem.at[0])
    load_x = pltpu.make_async_copy(xproj, px, lsem.at[1])
    load_t.start()
    load_x.start()

    barrier = pltpu.get_barrier_semaphore()
    greet = [z_peer] + [x_peer(i) for i in (1, 2, 3)]
    greet += [device(y_=(y + dy) % 4, c_=(c + dc) % 2) for dy, dc in yc]
    greet += [device(zl_=(zl + i) % 4) for i in (1, 2, 3)]
    greet += [yl_peer(dy, 1) for dy in (1, 2, 3)]
    for to in greet:
        pl.semaphore_signal(barrier, inc=1, device_id=to, device_id_type=MESH)
    emb[ft, 0] = table[...]
    emb[ft, 1] = text[...]
    pl.semaphore_wait(barrier, len(greet))

    def add_block(f, first=False):
        at = pl.ds(pl.multiple_of(f * width, 64), width)
        for side, proj in ((0, pt), (1, px)):
            term = matmul(emb[f, side], proj[at, :], (1, 0))
            z[side] = term if first else z[side] + term

    own = emb.at[ft]
    emb_z = post(own, own, slot("emb_z"), z_peer)
    emb_x = [post(own, own, slot("emb_x", i - 1), x_peer(i)) for i in (1, 2, 3)]
    load_t.wait()
    load_x.wait()
    add_block(ft, True)
    ft_z = (1 - zh) * 4 + x
    emb_z.wait_recv()
    far = emb.at[ft_z]
    emb_zx = [post(far, far, slot("emb_zx", i - 1), x_peer(i)) for i in (1, 2, 3)]
    add_block(ft_z)
    for i in (1, 3, 2):
        emb_x[i - 1].wait_recv()
        add_block(zh * 4 + (x + 4 - i) % 4)
    for i in (1, 3, 2):
        emb_zx[i - 1].wait_recv()
        add_block((1 - zh) * 4 + (x + 4 - i) % 4)

    def sum_dp(k, value):
        a, b = st_a.at[k], st_b.at[k]
        me_a, me_b = y * 2 + c, zl
        a[me_a] = value
        copies = [
            post(a.at[me_a], a.at[me_a], slot("st%d_a" % (k + 1), j),
                 device(y_=(y + dy) % 4, c_=(c + dc) % 2))
            for j, (dy, dc) in enumerate(yc)
        ]
        for copy in copies:
            copy.wait_recv()
        b[me_b] = jnp.sum(a[...], axis=0)
        copies = [
            post(b.at[me_b], b.at[me_b], slot("st%d_b" % (k + 1), i - 1), device(zl_=(zl + i) % 4))
            for i in (1, 2, 3)
        ]
        for copy in copies:
            copy.wait_recv()
        return jnp.sum(b[...], axis=0)

    def column(v):
        return jnp.sum(v, axis=0, keepdims=True)

    zero = jnp.zeros((4, feats), F32)
    zt, zx = z[0], z[1]
    total = sum_dp(0, jnp.concatenate(
        [column(zt), column(zt * zt), column(zx), column(zx * zx), zero], axis=0))
    inverse = []
    for side in (0, 1):
        center = total[2 * side:2 * side + 1] / pairs
        spread = total[2 * side + 1:2 * side + 2] / pairs - center * center
        inv = lax.rsqrt(spread + EPS)
        z[side] = (z[side] - center) * inv
        inverse.append(inv)
    me_p, me_g = y * 2 + l, l * 4 + y

    tab_g[me_p] = z[0].astype(BF16)
    half_full[ft] = z[1].astype(BF16)

    def a2a(f, j, go):
        local = jnp.logical_and(f % 4 == y, f // 4 == l)
        copy = pltpu.make_async_remote_copy(
            src_ref=half_full.at[f], dst_ref=txt_g.at[me_p],
            send_sem=ssem.at[slot("txt_a2a", j)], recv_sem=rsem.at[slot("txt_a2a") + me_p],
            device_id=device(y_=f % 4, zl_=h * 2 + f // 4), device_id_type=MESH,
        )

        @pl.when(jnp.logical_not(local))
        def _():
            if go:
                copy.start()
            else:
                copy.wait_send()

        if go:
            @pl.when(local)
            def _():
                txt_g[me_p] = half_full[f]

    own = half_full.at[ft]
    far = half_full.at[ft_z]
    txt_z = post(own, own, slot("txt_z"), z_peer)
    txt_x = [post(own, own, slot("txt_x", i - 1), x_peer(i)) for i in (1, 2, 3)]
    mine = tab_g.at[me_p]
    tab_l = post(mine, mine, slot("tab_l"), l_peer)
    tab_y = [post(mine, mine, slot("tab_y", i - 1), y_peer(i)) for i in (1, 2, 3)]
    order = [ft]
    a2a(ft, 0, True)
    txt_z.wait_recv()
    txt_zx = [post(far, far, slot("txt_zx", i - 1), x_peer(i)) for i in (1, 2, 3)]
    a2a(ft_z, 1, True)
    order.append(ft_z)
    tab_l.wait_recv()
    other = tab_g.at[y * 2 + 1 - l]
    tab_ly = [post(other, other, slot("tab_ly", i - 1), y_peer(i)) for i in (1, 2, 3)]
    for copies, zz in ((txt_x, zh), (txt_zx, 1 - zh)):
        for i in (1, 3, 2):
            copies[i - 1].wait_recv()
            f = zz * 4 + (x + 4 - i) % 4
            a2a(f, len(order), True)
            order.append(f)
    for copy in tab_y + tab_ly:
        copy.wait_recv()
    for j in range(1, 8):
        s = (me_p + j) % 8
        pltpu.make_async_remote_copy(
            src_ref=txt_g.at[s], dst_ref=txt_g.at[s], send_sem=ssem.at[slot("txt_a2a")],
            recv_sem=rsem.at[slot("txt_a2a") + s], device_id=l_peer, device_id_type=MESH,
        ).wait_recv()

    group = 8 * rows
    part[...] = matmul(tab_g[...].reshape(group, feats), txt_g[...].reshape(group, feats), (0, 0))
    at_c = pl.ds(pl.multiple_of((1 - c) * half, half), half)
    me_c = pl.ds(pl.multiple_of(c * half, half), half)
    post(part.at[at_c], part_c, slot("corr_c"), c_peer).wait_recv()
    row_index = ft * feats + c * half + lax.broadcasted_iota(jnp.int32, (half, feats), 0)
    col_index = me_g * feats + lax.broadcasted_iota(jnp.int32, (half, feats), 1)
    on_diag = row_index == col_index
    less = (part[me_c, :] + part_c[...]) / pairs - jnp.where(on_diag, 0.5, 0.0)
    part_h[...] = less.astype(BF16)
    part_c[...] = less
    post(part_h, part_hr, slot("corr_h"), h_peer).wait_recv()
    less = part_c[...] + part_hr[...].astype(F32)
    weighed = jnp.where(on_diag, less, OFF_WEIGHT * less)
    ker[me_c, :] = weighed.astype(BF16)
    ker_c = post(ker.at[me_c], ker.at[me_c], slot("ker_c"), c_peer)
    loss_part = 0.5 * column(weighed * less)
    ker_c.wait_recv()

    dxp[...] = matmul(tab_g[...].reshape(group, feats), ker[...], (1, 0)).astype(BF16).reshape(
        8, rows, feats)
    dx_a2a = [
        post(dxp.at[((y + dy) % 4) * 2 + (l + dl) % 2], dx.at[me_g], slot("dx_a2a", j), yl_peer(dy, dl))
        for j, (dy, dl) in enumerate(yl)
    ]
    dx[me_g] = dxp[me_p]

    def dx_on(g, j, go):
        copy = pltpu.make_async_remote_copy(
            src_ref=dx.at[g], dst_ref=dx_r.at[g // 4, x], send_sem=ssem.at[slot("dx_x", j)],
            recv_sem=rsem.at[slot("dx_x") + (g // 4) * 4 + x],
            device_id=device(x_=g % 4), device_id_type=MESH,
        )

        @pl.when(g % 4 != x)
        def _():
            if go:
                copy.start()
            else:
                copy.wait_send()

        if go:
            @pl.when(g % 4 == x)
            def _():
                dx_r[g // 4, x] = dx[g]

    dx_order = [me_g]
    dx_on(me_g, 0, True)

    dtp[...] = matmul(txt_g[...].reshape(group, feats), ker[...], (1, 1)).astype(BF16).reshape(
        8, rows, feats)
    dt_y = [
        post(dtp.at[pl.ds(((y + i) % 4) * 2, 2)], dt_r.at[i - 1], slot("dt_y", i - 1), y_peer(i))
        for i in (1, 2, 3)
    ]
    for j, (dy, dl) in enumerate(yl):
        dx_a2a[j].wait_recv()
        g = ((l + dl) % 2) * 4 + (y + 4 - dy) % 4
        dx_on(g, j + 1, True)
        dx_order.append(g)

    def dx_sum(zz):
        for i in (1, 2, 3):
            s = (x + i) % 4
            pltpu.make_async_remote_copy(
                src_ref=dx_r.at[zz, s], dst_ref=dx_r.at[zz, s], send_sem=ssem.at[slot("dx_x")],
                recv_sem=rsem.at[slot("dx_x") + zz * 4 + s], device_id=z_peer, device_id_type=MESH,
            ).wait_recv()
        return jnp.sum(dx_r[zz].astype(F32), axis=0)

    dx_far[...] = dx_sum(1 - zh).astype(BF16)
    dx_z = post(dx_far, dx_zr, slot("dx_z"), z_peer)

    for copy in dt_y:
        copy.wait_recv()

    def dt_sum(ll):
        total = dtp[y * 2 + ll].astype(F32)
        for i in range(3):
            total = total + dt_r[i, ll].astype(F32)
        return total

    dt_far[...] = dt_sum(1 - l).astype(BF16)
    dt_l = post(dt_far, dt_lr, slot("dt_l"), l_peer)
    d_table = dt_sum(l)
    d_text = dx_sum(zh)
    dt_l.wait_recv()
    d_table = d_table + dt_lr[...].astype(F32)
    dx_z.wait_recv()
    d_text = d_text + dx_zr[...].astype(F32)

    zt, zx = z[0], z[1]
    total = sum_dp(1, jnp.concatenate(
        [column(d_table), column(d_table * zt), column(d_text), column(d_text * zx),
         loss_part, zero[:3]], axis=0))
    back = []
    for side, d in ((0, d_table), (1, d_text)):
        mean = total[2 * side:2 * side + 1] / pairs
        tilt = total[2 * side + 1:2 * side + 2] / pairs
        back.append((inverse[side] * (d - mean - z[side] * tilt)).astype(BF16))

    ls_x[0] = jnp.broadcast_to(jnp.sum(total[4:5], axis=1, keepdims=True), (8, 128))
    ls_copies = [post(ls_x.at[0], ls_x.at[i], slot("loss_x", i - 1), x_peer(i)) for i in (1, 2, 3)]

    copies = {}
    for k, zz in ((0, 1 - zh), (1, zh)):
        for i in (1, 3, 2, 0):
            f = zz * 4 + (x + i) % 4
            at = pl.ds(pl.multiple_of(f * width, 64), width)
            for side, proj in ((0, pt), (1, px)):
                term = matmul(back[side], proj[at, :], (1, 1))
                if i:
                    gp[k, i - 1, side] = term.astype(BF16)
                else:
                    g_own[k, side] = term
            if i:
                copies[k, i] = post(
                    gp.at[k, i - 1], gr.at[k, i - 1],
                    slot("gr_far" if k == 0 else "gr_near", i - 1), x_peer(i))

    def gr_sum(k, side):
        total = g_own[k, side]
        for i in range(3):
            total = total + gr[k, i, side].astype(F32)
        return total

    for copy in ls_copies:
        copy.wait_recv()
    ls_z[0] = jnp.sum(ls_x[...], axis=0)
    ls_copy = post(ls_z.at[0], ls_z.at[1], slot("loss_z"), z_peer)
    for i in (1, 3, 2):
        copies[0, i].wait_recv()
    for side in (0, 1):
        g_far[side] = gr_sum(0, side).astype(BF16)
    gr_z = post(g_far, g_zr, slot("gr_z"), z_peer)
    ls_copy.wait_recv()
    loss_out[...] = (ls_z[0] + ls_z[1]) / (feats * NUM_FEAT)
    for i in (1, 3, 2):
        copies[1, i].wait_recv()
    gr_z.wait_recv()
    grad_table[...] = gr_sum(1, 0) + g_zr[0].astype(F32)
    grad_text[...] = gr_sum(1, 1) + g_zr[1].astype(F32)

    for copy in started:
        copy.wait_send()
    for j, f in enumerate(order):
        a2a(f, j, False)
    for j, g in enumerate(dx_order):
        dx_on(g, j, False)


def body(table, text, table_proj, text_proj):
    rows, width = table.shape
    depth, feats = table_proj.shape
    half = feats // 2
    vmem = pl.BlockSpec(memory_space=pltpu.VMEM)
    hbm = pl.BlockSpec(memory_space=pl.ANY)
    v = pltpu.VMEM
    grad_table, grad_text, loss = pl.pallas_call(
        kernel,
        out_shape=(
            jax.ShapeDtypeStruct((rows, width), F32),
            jax.ShapeDtypeStruct((rows, width), F32),
            jax.ShapeDtypeStruct((8, 128), F32),
        ),
        in_specs=[vmem, vmem, hbm, hbm],
        out_specs=(vmem, vmem, vmem),
        scratch_shapes=[
            v((depth, feats), BF16), v((depth, feats), BF16),
            v((NUM_FEAT, 2, rows, width), BF16),
            v((2, rows, feats), F32),
            v((2, 8, 8, feats), F32), v((2, 4, 8, feats), F32),
            v((NUM_FEAT, rows, feats), BF16),
            v((8, rows, feats), BF16), v((8, rows, feats), BF16),
            v((feats, feats), F32), v((half, feats), F32),
            v((half, feats), BF16), v((half, feats), BF16),
            v((feats, feats), BF16),
            v((8, rows, feats), BF16), v((8, rows, feats), BF16),
            v((2, 4, rows, feats), BF16),
            v((rows, feats), BF16), v((rows, feats), BF16),
            v((8, rows, feats), BF16), v((3, 2, rows, feats), BF16),
            v((rows, feats), BF16), v((rows, feats), BF16),
            v((2, 3, 2, rows, width), BF16), v((2, 3, 2, rows, width), BF16),
            v((2, 2, rows, width), F32),
            v((2, rows, width), BF16), v((2, rows, width), BF16),
            v((4, 8, 128), F32), v((2, 8, 128), F32),
            pltpu.SemaphoreType.DMA((NUM_SLOTS,)),
            pltpu.SemaphoreType.DMA((NUM_SLOTS,)),
            pltpu.SemaphoreType.DMA((2,)),
        ],
        compiler_params=pltpu.CompilerParams(
            collective_id=0, has_side_effects=True, vmem_limit_bytes=56 * 1024 * 1024
        ),
        cost_estimate=pl.CostEstimate(flops=3_500_000_000, bytes_accessed=9_000_000, transcendentals=2048),
        name="barlow_step",
    )(table, text, table_proj, text_proj)
    return (grad_table, grad_text, loss[0, :1])


def solution(mesh):
    placed = (P("dp", "feat"), P("dp", "feat"), P(None, "feat"), P(None, "feat"))
    return jax.shard_map(
        body,
        mesh=mesh,
        in_specs=placed,
        out_specs=(P("dp", "feat"), P("dp", "feat"), P()),
        check_vma=False,
    )
```

```python
import jax
import jax.numpy as jnp
from jax import lax
from jax.experimental import pallas as pl
from jax.experimental.pallas import tpu as pltpu
from jax.sharding import PartitionSpec as P

OFF_WEIGHT = 0.1
EPS = 1e-05
MESH = pl.DeviceIdType.MESH
BF16, F32 = jnp.bfloat16, jnp.float32
NUM_DP, NUM_FEAT = 32, 8
TABLE, TEXT = 0, 1
FAR, NEAR = 0, 1
LANES = 128

SLOTS = {}
for _name, _count in (
    ("emb_z", 2), ("emb_x", 16),
    ("st_a", 28), ("st_b", 12),
    ("txt_z", 1), ("txt_x", 8), ("txt_a2a", 8),
    ("tab_c", 4), ("tab_y", 4),
    ("corr_l", 2), ("corr_h", 2), ("ker_l", 2),
    ("dx_a2a", 16), ("dx_x", 12), ("dx_z", 2),
    ("dt_y", 6), ("dt_c", 1),
    ("gr_x", 24), ("gr_z", 2),
    ("loss_x", 3), ("loss_z", 1),
):
    SLOTS[_name] = (sum(n for _, n in SLOTS.values()), _count)
NUM_SLOTS = sum(n for _, n in SLOTS.values())


def slot(name, i=0):
    return SLOTS[name][0] + i


def matmul(a, b, dims):
    return lax.dot_general(a, b, ((dims[:1], dims[1:]), ((), ())), preferred_element_type=F32)


def column(v):
    return jnp.sum(v, axis=0, keepdims=True)


def fold(v):
    n = v.shape[1] // LANES
    return jnp.concatenate([v[:, i * LANES:(i + 1) * LANES] for i in range(n)], axis=0)


def unfold(v):
    return jnp.concatenate([v[i:i + 1] for i in range(v.shape[0])], axis=1)


class Gather:
    def __init__(self, post, base, peer, block):
        self.post, self.base, self.peer, self.block = post, base, peer, block

    def start(self):
        own = self.block(0)
        self.from_left = self.post(own, own, self.base, self.peer(1))
        self.from_right = self.post(own, own, self.base + 1, self.peer(3))

    def relay_left(self):
        self.from_left.wait_recv()
        part = self.block(3, 0)
        self.half_left = self.post(part, part, self.base + 2, self.peer(1))

    def relay_right(self):
        self.from_right.wait_recv()
        part = self.block(1, 1)
        self.half_right = self.post(part, part, self.base + 3, self.peer(3))

    def finish(self):
        self.half_left.wait_recv()
        self.half_right.wait_recv()


class Reduce:
    def __init__(self, post, base, peer, src, val, buf):
        self.post, self.base, self.peer, self.src, self.val, self.buf = post, base, peer, src, val, buf
        self.relayed, self.direct, self.final_copy = {}, {}, {}

    def send_opposite(self, half):
        to = (1, 3)[half]
        self.relayed[half] = self.post(
            self.src(2, half), self.buf.at[0, half], self.base + half, self.peer(to))

    def send_direct(self, half):
        to = (3, 1)[half]
        self.direct[half] = self.post(
            self.src(to, half), self.buf.at[1, half], self.base + 2 + half, self.peer(to))

    def pass_on(self, half):
        to = (1, 3)[half]
        self.relayed[half].wait_recv()
        self.buf[2, half] = (self.buf[0, half].astype(F32) + self.val(to, half)).astype(BF16)
        self.final_copy[half] = self.post(
            self.buf.at[2, half], self.buf.at[3, half], self.base + 4 + half, self.peer(to))

    def total(self, half):
        self.direct[half].wait_recv()
        self.final_copy[half].wait_recv()
        return self.val(0, half) + self.buf[1, half].astype(F32) + self.buf[3, half].astype(F32)


def kernel(
    table, text, tproj, xproj,
    grad_table, grad_text, loss_out,
    pt, px, emb, z, st_a, st_b, half_full, tab_g, txt_g,
    part, part_s, part_r, part_h, part_hr, ker,
    dxp, dx, dx_buf, dx_far, dx_zr, dtp, dt_cr, dt_half, dt_buf, d,
    gp, g_own, gr_buf, g_far, g_zr, ls_x, ls_z,
    ssem, rsem, lsem,
):
    width, rows = table.shape
    feats = tproj.shape[1]
    pairs = rows * NUM_DP
    half = feats // 2
    low, mid = rows // 2, width // 2
    projs = (pt, px)
    dp, ft = lax.axis_index("dp"), lax.axis_index("feat")
    zl, y, c = dp // 8, (dp // 2) % 4, dp % 2
    h, l = zl // 2, zl % 2
    zh, x = ft // 4, ft % 4
    me_p, me_g = y * 2 + c, c * 4 + y

    def device(zl_=zl, y_=y, c_=c, zh_=zh, x_=x):
        return {"dp": (zl_ * 4 + y_) * 2 + c_, "feat": zh_ * 4 + x_}

    z_peer = device(zh_=1 - zh)
    c_peer = device(c_=1 - c)
    l_peer = device(zl_=h * 2 + 1 - l)
    h_peer = device(zl_=(1 - h) * 2 + l)

    def x_peer(i):
        return device(x_=(x + i) % 4)

    def y_peer(i):
        return device(y_=(y + i) % 4)

    yc = [(dy, dc) for dy in range(4) for dc in range(2) if dy or dc]

    def yc_peer(dy, dc):
        return device(y_=(y + dy) % 4, c_=(c + dc) % 2)

    def zl_peer(i):
        return device(zl_=(zl + i) % 4)

    drain = []

    def remote(src, dst, s, to, r=None):
        return pltpu.make_async_remote_copy(
            src_ref=src, dst_ref=dst, send_sem=ssem.at[s], recv_sem=rsem.at[s if r is None else r],
            device_id=to, device_id_type=MESH,
        )

    def post(src, dst, s, to, r=None):
        copy = remote(src, dst, s, to, r)
        copy.start()
        drain.append(copy.wait_send)
        return copy

    loads = [
        pltpu.make_async_copy(a, b, lsem.at[i])
        for i, (a, b) in enumerate(
            ((table, emb.at[ft, TABLE]), (text, emb.at[ft, TEXT]), (tproj, pt), (xproj, px)))
    ]
    for i in (1, 0, 3, 2):
        loads[i].start()

    barrier = pltpu.get_barrier_semaphore()
    greet = [z_peer] + [x_peer(i) for i in (1, 2, 3)]
    greet += [yc_peer(*k) for k in yc] + [zl_peer(i) for i in (1, 2, 3)]
    for to in greet:
        pl.semaphore_signal(barrier, inc=1, device_id=to, device_id_type=MESH)
    loads[1].wait()
    loads[0].wait()
    pl.semaphore_wait(barrier, len(greet))

    def feat(zz, k):
        return zz * 4 + (x + k) % 4

    zf = 1 - zh
    ft_z = feat(zf, 0)

    def add_block(side, f, first=False):
        at = pl.ds(pl.multiple_of(f * width, 64), width)
        term = matmul(emb[f, side], projs[side][at, :], (0, 0))
        z[side] = term if first else z[side] + term

    def emb_gather(side, where):
        def block(k, part_=None):
            f = feat((zf, zh)[where], k)
            return emb.at[f, side] if part_ is None else emb.at[f, side, pl.ds(part_ * mid, mid)]

        return Gather(post, slot("emb_x", (side * 2 + where) * 4), x_peer, block)

    def emb_send_z(side):
        own = emb.at[ft, side]
        return post(own, own, slot("emb_z", side), z_peer)

    def emb_relay(g, side, zz):
        g.relay_left()
        g.relay_right()
        add_block(side, feat(zz, 3))
        add_block(side, feat(zz, 1))

    stats = {}

    def stat_a(k, value):
        n = value.shape[0]
        a = st_a.at[k, me_p, pl.ds(0, n)]
        a[...] = value
        stats[k, 0] = n, [
            post(a, a, slot("st_a", k * 7 + j), yc_peer(*to)) for j, to in enumerate(yc)]

    def stat_b(k):
        n, copies = stats[k, 0]
        for copy in copies:
            copy.wait_recv()
        b = st_b.at[k, zl, pl.ds(0, n)]
        b[...] = jnp.sum(st_a[k, :, :n], axis=0)
        stats[k, 1] = [
            post(b, b, slot("st_b", k * 3 + i - 1), zl_peer(i)) for i in (1, 2, 3)]

    def stat_c(k):
        for copy in stats[k, 1]:
            copy.wait_recv()
        return jnp.sum(st_b[k, :, :stats[k, 0][0]], axis=0)

    def forward_stats(side):
        v = z[side]
        stat_a(side, jnp.concatenate([fold(column(v)), fold(column(v * v))], axis=0))

    lanes = feats // LANES

    def forward_normalize(side):
        total = stat_c(side)
        center = unfold(total[:lanes]) / pairs
        spread = unfold(total[lanes:2 * lanes]) / pairs - center * center
        inv = lax.rsqrt(spread + EPS)
        z[side] = (z[side] - center) * inv
        return inv

    emb_zx = emb_send_z(TEXT)
    xn = emb_gather(TEXT, NEAR)
    xn.start()
    loads[3].wait()
    add_block(TEXT, ft, True)
    emb_zt = emb_send_z(TABLE)
    emb_relay(xn, TEXT, zh)
    emb_zx.wait_recv()
    xf = emb_gather(TEXT, FAR)
    xf.start()
    tn = emb_gather(TABLE, NEAR)
    tn.start()
    add_block(TEXT, ft_z)
    loads[2].wait()
    add_block(TABLE, ft, True)
    xn.finish()
    add_block(TEXT, feat(zh, 2))
    emb_relay(xf, TEXT, zf)
    emb_relay(tn, TABLE, zh)
    emb_zt.wait_recv()
    tf = emb_gather(TABLE, FAR)
    tf.start()
    add_block(TABLE, ft_z)
    xf.finish()
    add_block(TEXT, feat(zf, 2))
    forward_stats(TEXT)
    tn.finish()
    add_block(TABLE, feat(zh, 2))
    emb_relay(tf, TABLE, zf)
    stat_b(TEXT)
    tf.finish()
    add_block(TABLE, feat(zf, 2))
    forward_stats(TABLE)
    inv_text = forward_normalize(TEXT)

    half_full[ft] = z[TEXT].astype(BF16)

    def a2a(f, j):
        local = jnp.logical_and(f % 4 == y, f // 4 == c)
        copy = remote(
            half_full.at[f], txt_g.at[me_p], slot("txt_a2a", j),
            device(y_=f % 4, c_=f // 4), slot("txt_a2a") + me_p)

        @pl.when(jnp.logical_not(local))
        def _():
            copy.start()

        @pl.when(local)
        def _():
            txt_g[me_p] = half_full[f]

        def wait():
            @pl.when(jnp.logical_not(local))
            def _():
                copy.wait_send()

        drain.append(wait)

    def txt_gather(where):
        def block(k, part_=None):
            f = feat((zf, zh)[where], k)
            return half_full.at[f] if part_ is None else half_full.at[f, pl.ds(part_ * low, low)]

        return Gather(post, slot("txt_x", where * 4), x_peer, block)

    def tab_block(k, part_=None):
        p = ((y + k) % 4) * 2 + c
        return tab_g.at[p] if part_ is None else tab_g.at[p, pl.ds(part_ * low, low)]

    def tab_share(k):
        return post(tab_block(k), tab_block(k), slot("tab_c", k), c_peer)

    own = half_full.at[ft]
    txt_z = post(own, own, slot("txt_z"), z_peer)
    cn = txt_gather(NEAR)
    cn.start()
    a2a(ft, 0)
    stat_b(TABLE)
    cn.relay_left()
    a2a(feat(zh, 3), 1)
    cn.relay_right()
    a2a(feat(zh, 1), 2)
    inv_table = forward_normalize(TABLE)
    tab_g[me_p] = z[TABLE].astype(BF16)
    hn = Gather(post, slot("tab_y"), y_peer, tab_block)
    hn.start()
    shared = [tab_share(0)]
    txt_z.wait_recv()
    cf = txt_gather(FAR)
    cf.start()
    a2a(ft_z, 3)
    cn.finish()
    a2a(feat(zh, 2), 4)
    hn.relay_left()
    shared.append(tab_share(3))
    hn.relay_right()
    shared.append(tab_share(1))
    cf.relay_left()
    a2a(feat(zf, 3), 5)
    cf.relay_right()
    a2a(feat(zf, 1), 6)
    hn.finish()
    shared.append(tab_share(2))
    cf.finish()
    a2a(feat(zf, 2), 7)
    for copy in shared:
        copy.wait_recv()
    for j in range(1, 8):
        s = (me_p + j) % 8
        remote(txt_g.at[s], txt_g.at[s], slot("txt_a2a"), c_peer, slot("txt_a2a") + s).wait_recv()

    group = 8 * rows
    tabs = tab_g[...].reshape(group, feats)
    at_l = pl.ds(pl.multiple_of((1 - l) * half, half), half)
    me_l = pl.ds(pl.multiple_of(l * half, half), half)
    chunks = [slice(0, half), slice(half, feats)]
    corr_l = []
    for k, cols in enumerate(chunks):
        row_index = ft * feats + lax.broadcasted_iota(jnp.int32, (feats, half), 0)
        col_index = me_g * feats + k * half + lax.broadcasted_iota(jnp.int32, (feats, half), 1)
        part[k] = matmul(tabs, txt_g[:, :, cols].reshape(group, half), (0, 0)) / pairs - jnp.where(
            row_index == col_index, 0.25, 0.0)
        part_s[k] = part[k, at_l, :].astype(BF16)
        corr_l.append(post(part_s.at[k], part_r.at[k], slot("corr_l", k), l_peer))
    corr_h = []
    for k in (0, 1):
        corr_l[k].wait_recv()
        less = part[k, me_l, :] + part_r[k].astype(F32)
        part_h[k] = less.astype(BF16)
        part[k, me_l, :] = less
        corr_h.append(post(part_h.at[k], part_hr.at[k], slot("corr_h", k), h_peer))

    loss_part = None
    for k in (0, 1):
        corr_h[k].wait_recv()
        less = part[k, me_l, :] + part_hr[k].astype(F32)
        row_index = ft * feats + l * half + lax.broadcasted_iota(jnp.int32, (half, half), 0)
        col_index = me_g * feats + k * half + lax.broadcasted_iota(jnp.int32, (half, half), 1)
        weighed = jnp.where(row_index == col_index, less, OFF_WEIGHT * less)
        ker[k, me_l, :] = weighed.astype(BF16)
        mine = ker.at[k, me_l]
        ker_l = post(mine, mine, slot("ker_l", k), l_peer)
        loss_k = column(0.5 * weighed * less)
        loss_part = loss_k if loss_part is None else loss_part + loss_k
        ker_l.wait_recv()
        dxp[k] = matmul(tab_g[...].reshape(group, feats), ker[k], (1, 0)).astype(BF16).reshape(
            8, rows, half)
        for j, (dy, dc) in enumerate(yc):
            post(dxp.at[k, ((y + dy) % 4) * 2 + (c + dc) % 2], dx.at[k, me_g],
                 slot("dx_a2a", k * 8 + j), yc_peer(dy, dc), slot("dx_a2a") + k * 8 + me_g)
        dx[k, me_g] = dxp[k, me_p]

    def dx_wait(k, g):
        @pl.when(g != me_g)
        def _():
            remote(dx.at[k, g], dx.at[k, g], slot("dx_a2a"), z_peer, slot("dx_a2a") + k * 8 + g).wait_recv()

    txts = txt_g[...].reshape(group, feats)
    both = (
        matmul(txts[:, chunks[0]], ker[0], (1, 1)) + matmul(txts[:, chunks[1]], ker[1], (1, 1))
    ).reshape(4, 2, rows, feats)
    for k in (0, 1):
        dtp[k] = both[:, k]
    dt_c = post(dtp.at[1 - c], dt_cr, slot("dt_c"), c_peer)

    def dt_src(k, part_):
        return dt_half.at[(y + k) % 4, pl.ds(part_ * low, low)]

    def dt_val(k, part_):
        return dt_cr[(y + k) % 4, part_ * low:(part_ + 1) * low, :]

    dt = Reduce(post, slot("dt_y"), y_peer, dt_src, dt_val, dt_buf)

    def dt_start():
        dt_c.wait_recv()
        for k in (2, 3, 1, 0):
            at = (y + k) % 4
            total = dtp[c, at] + dt_cr[at]
            dt_cr[at] = total
            dt_half[at] = total.astype(BF16)
            if k == 2:
                dt.send_opposite(0)
                dt.send_opposite(1)
            elif k:
                dt.send_direct(0 if k == 3 else 1)

    def dx_reduce(where):
        def src(k, part_):
            return dx.at[part_, feat((zf, zh)[where], k)]

        return Reduce(post, slot("dx_x", where * 6), x_peer, src,
                      lambda k, part_: src(k, part_)[...].astype(F32), dx_buf.at[where])

    dxr = [dx_reduce(FAR), dx_reduce(NEAR)]
    for k in (0, 1):
        if k == 1:
            dt_start()
        for r, zz in zip(dxr, (zf, zh)):
            dx_wait(k, feat(zz, 2))
            r.send_opposite(k)
            dx_wait(k, feat(zz, (3, 1)[k]))
            r.send_direct(k)
        for r, zz in zip(dxr, (zf, zh)):
            dx_wait(k, feat(zz, (1, 3)[k]))
            r.pass_on(k)
            dx_wait(k, feat(zz, 0))
    dt.pass_on(0)
    dt.pass_on(1)
    dx_z = []
    for k in (0, 1):
        dx_far[k] = dxr[FAR].total(k).astype(BF16)
        dx_z.append(post(dx_far.at[k], dx_zr.at[k], slot("dx_z", k), z_peer))
    for k in (0, 1):
        d[TABLE, pl.ds(k * low, low)] = dt.total(k)

    def backward_stats(side, extra=None):
        v = d[side]
        parts = [fold(column(v)), fold(column(v * z[side]))]
        if extra is not None:
            parts += [fold(extra), jnp.zeros((lanes, LANES), F32)]
        stat_a(2 + side, jnp.concatenate(parts, axis=0))

    def backward(side, inv):
        total = stat_c(2 + side)
        mean = unfold(total[:lanes]) / pairs
        tilt = unfold(total[lanes:2 * lanes]) / pairs
        return (inv * (d[side] - mean - z[side] * tilt)).astype(BF16), total

    backward_stats(TABLE, loss_part)
    for k, cols in enumerate(chunks):
        v = dxr[NEAR].total(k)
        dx_z[k].wait_recv()
        d[TEXT, :, cols] = v + dx_zr[k].astype(F32)
    stat_b(2 + TABLE)
    backward_stats(TEXT)

    def grad_reduce(side, where):
        def src(k, part_):
            return gp.at[side, where, k, pl.ds(part_ * mid, mid)]

        def val(k, part_):
            return g_own[side, where, k, part_ * mid:(part_ + 1) * mid, :]

        return Reduce(post, slot("gr_x", (side * 2 + where) * 6), x_peer, src, val,
                      gr_buf.at[side, where])

    def grad_terms(side, where, back, r):
        for k in (2, 3, 1, 0):
            at = pl.ds(pl.multiple_of(feat((zf, zh)[where], k) * width, 64), width)
            term = matmul(projs[side][at, :], back, (1, 1))
            if k:
                gp[side, where, k] = term.astype(BF16)
            if k != 2:
                g_own[side, where, k] = term
            if k == 2:
                r.send_opposite(0)
                r.send_opposite(1)
            elif k:
                r.send_direct(0 if k == 3 else 1)

    gr = [[grad_reduce(s, w) for w in (FAR, NEAR)] for s in (TABLE, TEXT)]
    grad_z = [None, None]

    def grad_far(side):
        for k in (0, 1):
            g_far[side, pl.ds(k * mid, mid)] = gr[side][FAR].total(k).astype(BF16)
        grad_z[side] = post(g_far.at[side], g_zr.at[side], slot("gr_z", side), z_peer)

    def grad_pass(side, where):
        gr[side][where].pass_on(0)
        gr[side][where].pass_on(1)

    back_table, total = backward(TABLE, inv_table)
    grad_terms(TABLE, FAR, back_table, gr[TABLE][FAR])
    stat_b(2 + TEXT)
    grad_terms(TABLE, NEAR, back_table, gr[TABLE][NEAR])
    ls_x[0] = jnp.broadcast_to(
        column(jnp.sum(total[2 * lanes:3 * lanes], axis=1, keepdims=True)), (8, LANES))
    ls_copies = [post(ls_x.at[0], ls_x.at[i], slot("loss_x", i - 1), x_peer(i)) for i in (1, 2, 3)]
    grad_pass(TABLE, FAR)
    back_text, _ = backward(TEXT, inv_text)
    grad_terms(TEXT, FAR, back_text, gr[TEXT][FAR])
    grad_far(TABLE)
    grad_pass(TABLE, NEAR)
    grad_terms(TEXT, NEAR, back_text, gr[TEXT][NEAR])
    grad_pass(TEXT, FAR)
    for copy in ls_copies:
        copy.wait_recv()
    ls_z[0] = jnp.sum(ls_x[...], axis=0)
    ls_copy = post(ls_z.at[0], ls_z.at[1], slot("loss_z"), z_peer)
    grad_far(TEXT)
    grad_pass(TEXT, NEAR)

    def grad_near(side, out):
        near = [gr[side][NEAR].total(k) for k in (0, 1)]
        grad_z[side].wait_recv()
        for k in (0, 1):
            at = slice(k * mid, (k + 1) * mid)
            out[at, :] = near[k] + g_zr[side, at, :].astype(F32)

    grad_near(TABLE, grad_table)
    ls_copy.wait_recv()
    loss_out[...] = ((ls_z[0] + ls_z[1]) / (feats * NUM_FEAT))[:1, :1]
    grad_near(TEXT, grad_text)
    for wait in drain:
        wait()


def body(table, text, table_proj, text_proj):
    rows, width = table.shape
    depth, feats = table_proj.shape
    half, low = feats // 2, rows // 2
    vmem = pl.BlockSpec(memory_space=pltpu.VMEM)
    hbm = pl.BlockSpec(memory_space=pl.ANY)
    v = pltpu.VMEM
    grad_table, grad_text, loss = pl.pallas_call(
        kernel,
        out_shape=(
            jax.ShapeDtypeStruct((width, rows), F32),
            jax.ShapeDtypeStruct((width, rows), F32),
            jax.ShapeDtypeStruct((1, 1), F32),
        ),
        in_specs=[hbm, hbm, hbm, hbm],
        out_specs=(vmem, vmem, vmem),
        scratch_shapes=[
            v((depth, feats), BF16), v((depth, feats), BF16),
            v((NUM_FEAT, 2, width, rows), BF16),
            v((2, rows, feats), F32),
            v((4, 8, 16, LANES), F32), v((4, 4, 16, LANES), F32),
            v((NUM_FEAT, rows, feats), BF16),
            v((8, rows, feats), BF16), v((8, rows, feats), BF16),
            v((2, feats, half), F32),
            v((2, half, half), BF16), v((2, half, half), BF16),
            v((2, half, half), BF16), v((2, half, half), BF16),
            v((2, feats, half), BF16),
            v((2, 8, rows, half), BF16), v((2, 8, rows, half), BF16),
            v((2, 4, 2, rows, half), BF16),
            v((2, rows, half), BF16), v((2, rows, half), BF16),
            v((2, 4, rows, feats), F32), v((4, rows, feats), F32),
            v((4, rows, feats), BF16), v((4, 2, low, feats), BF16),
            v((2, rows, feats), F32),
            v((2, 2, 4, width, rows), BF16), v((2, 2, 4, width, rows), F32),
            v((2, 2, 4, 2, width // 2, rows), BF16),
            v((2, width, rows), BF16), v((2, width, rows), BF16),
            v((4, 8, LANES), F32), v((2, 8, LANES), F32),
            pltpu.SemaphoreType.DMA((NUM_SLOTS,)),
            pltpu.SemaphoreType.DMA((NUM_SLOTS,)),
            pltpu.SemaphoreType.DMA((4,)),
        ],
        compiler_params=pltpu.CompilerParams(
            collective_id=0, has_side_effects=True, vmem_limit_bytes=56 * 1024 * 1024
        ),
        cost_estimate=pl.CostEstimate(flops=3_500_000_000, bytes_accessed=9_000_000, transcendentals=2048),
        name="barlow_step",
    )(table.T, text.T, table_proj, text_proj)
    return (grad_table.T, grad_text.T, loss.reshape(1))


def solution(mesh):
    placed = (P("dp", "feat"), P("dp", "feat"), P(None, "feat"), P(None, "feat"))
    return jax.shard_map(
        body,
        mesh=mesh,
        in_specs=placed,
        out_specs=(P("dp", "feat"), P("dp", "feat"), P()),
        check_vma=False,
    )
```

```python
import jax
import jax.numpy as jnp
from jax import lax
from jax.experimental import pallas as pl
from jax.experimental.pallas import tpu as pltpu
from jax.sharding import PartitionSpec as P

OFF_WEIGHT = 0.1
EPS = 1e-05
MESH = pl.DeviceIdType.MESH
BF16, F32 = jnp.bfloat16, jnp.float32
NUM_DP, NUM_FEAT = 32, 8
TABLE, TEXT = 0, 1
CHUNKS = 2
FAR, NEAR = 0, 1
LANES = 128

SLOTS = {}
for _name, _count in (
    ("emb_z", 2), ("emb_x", 16),
    ("st_a", 14), ("st_b", 6),
    ("half_sum", 3), ("bt_a", 7), ("bt_b", 3), ("bx_l", 1), ("bx_x", 3), ("bx_z", 1), ("bx_y", 7),
    ("txt_z", 1), ("txt_x", 8), ("txt_a2a", 8),
    ("tab_c", 4), ("tab_y", 4),
    ("corr_l", CHUNKS), ("corr_h", CHUNKS), ("ker_l", CHUNKS),
    ("dx_a2a", CHUNKS * 8), ("dx_x", 12), ("dx_z", 2),
    ("dt_y", 6), ("dt_c", 1),
    ("gr_x", 24), ("gr_z", 2),
    ("loss_x", 3), ("loss_z", 1),
):
    SLOTS[_name] = (sum(n for _, n in SLOTS.values()), _count)
NUM_SLOTS = sum(n for _, n in SLOTS.values())


def slot(name, i=0):
    return SLOTS[name][0] + i


def matmul(a, b, dims):
    return lax.dot_general(a, b, ((dims[:1], dims[1:]), ((), ())), preferred_element_type=F32)


def split(v):
    high = v.astype(BF16)
    return high, (v - high.astype(F32)).astype(BF16)


def rows_of(v):
    high, low = split(v)
    return jnp.concatenate([high, low, jnp.zeros((14, v.shape[1]), BF16)], axis=0)


def column(v):
    return jnp.sum(v, axis=0, keepdims=True)


def fold(v):
    n = v.shape[1] // LANES
    return jnp.concatenate([v[:, i * LANES:(i + 1) * LANES] for i in range(n)], axis=0)


def unfold(v):
    return jnp.concatenate([v[i:i + 1] for i in range(v.shape[0])], axis=1)


class Gather:
    def __init__(self, post, base, peer, block):
        self.post, self.base, self.peer, self.block = post, base, peer, block

    def start(self):
        own = self.block(0)
        self.from_left = self.post(own, own, self.base, self.peer(1))
        self.from_right = self.post(own, own, self.base + 1, self.peer(3))

    def relay_left(self):
        self.from_left.wait_recv()
        part = self.block(3, 0)
        self.half_left = self.post(part, part, self.base + 2, self.peer(1))

    def relay_right(self):
        self.from_right.wait_recv()
        part = self.block(1, 1)
        self.half_right = self.post(part, part, self.base + 3, self.peer(3))

    def finish(self):
        self.half_left.wait_recv()
        self.half_right.wait_recv()


class Reduce:
    def __init__(self, post, base, peer, src, val, buf):
        self.post, self.base, self.peer, self.src, self.val, self.buf = post, base, peer, src, val, buf
        self.relayed, self.direct, self.final_copy = {}, {}, {}

    def send_opposite(self, half):
        to = (1, 3)[half]
        self.relayed[half] = self.post(
            self.src(2, half), self.buf.at[0, half], self.base + half, self.peer(to))

    def send_direct(self, half):
        to = (3, 1)[half]
        self.direct[half] = self.post(
            self.src(to, half), self.buf.at[1, half], self.base + 2 + half, self.peer(to))

    def pass_on(self, half):
        to = (1, 3)[half]
        self.relayed[half].wait_recv()
        self.buf[2, half] = (self.buf[0, half].astype(F32) + self.val(to, half)).astype(BF16)
        self.final_copy[half] = self.post(
            self.buf.at[2, half], self.buf.at[3, half], self.base + 4 + half, self.peer(to))

    def total(self, half):
        self.direct[half].wait_recv()
        self.final_copy[half].wait_recv()
        return self.val(0, half) + self.buf[1, half].astype(F32) + self.buf[3, half].astype(F32)


def kernel(
    table, text, tproj, xproj,
    grad_table, grad_text, loss_out,
    pt, px, emb, z, st_a, st_b, half_full, tab_g, txt_g,
    part, part_s, part_r, part_h, part_hr, ker,
    dxp, dx, dx_buf, dx_far, dx_zr, dtp, dt_cr, dt_half, dt_buf, d,
    gp, g_own, gr_buf, g_far, g_zr, ls_x, ls_z,
    halves, bt_a, bt_b, bx_l, bx_x, bx_z, bx_y,
    ssem, rsem, lsem,
):
    width, rows = table.shape
    feats = tproj.shape[1]
    pairs = rows * NUM_DP
    half = feats // 2
    low, mid = rows // 2, width // 2
    projs = (pt, px)
    dp, ft = lax.axis_index("dp"), lax.axis_index("feat")
    zl, y, c = dp // 8, (dp // 2) % 4, dp % 2
    h, l = zl // 2, zl % 2
    zh, x = ft // 4, ft % 4
    me_p, me_g = y * 2 + c, c * 4 + y

    def device(zl_=zl, y_=y, c_=c, zh_=zh, x_=x):
        return {"dp": (zl_ * 4 + y_) * 2 + c_, "feat": zh_ * 4 + x_}

    z_peer = device(zh_=1 - zh)
    c_peer = device(c_=1 - c)
    l_peer = device(zl_=h * 2 + 1 - l)
    h_peer = device(zl_=(1 - h) * 2 + l)

    def x_peer(i):
        return device(x_=(x + i) % 4)

    def y_peer(i):
        return device(y_=(y + i) % 4)

    yc = [(dy, dc) for dy in range(4) for dc in range(2) if dy or dc]

    def yc_peer(dy, dc):
        return device(y_=(y + dy) % 4, c_=(c + dc) % 2)

    def zl_peer(i):
        return device(zl_=(zl + i) % 4)

    drain = []

    def remote(src, dst, s, to, r=None):
        return pltpu.make_async_remote_copy(
            src_ref=src, dst_ref=dst, send_sem=ssem.at[s], recv_sem=rsem.at[s if r is None else r],
            device_id=to, device_id_type=MESH,
        )

    def post(src, dst, s, to, r=None):
        copy = remote(src, dst, s, to, r)
        copy.start()
        drain.append(copy.wait_send)
        return copy

    loads = [
        pltpu.make_async_copy(a, b, lsem.at[i])
        for i, (a, b) in enumerate(
            ((table, emb.at[ft, TABLE]), (text, emb.at[ft, TEXT]), (tproj, pt), (xproj, px)))
    ]
    for i in (1, 0, 3, 2):
        loads[i].start()

    barrier = pltpu.get_barrier_semaphore()
    greet = [z_peer] + [x_peer(i) for i in (1, 2, 3)]
    greet += [yc_peer(*k) for k in yc] + [zl_peer(i) for i in (1, 2, 3)]
    for to in greet:
        pl.semaphore_signal(barrier, inc=1, device_id=to, device_id_type=MESH)
    loads[1].wait()
    loads[0].wait()
    pl.semaphore_wait(barrier, len(greet))

    def feat(zz, k):
        return zz * 4 + (x + k) % 4

    zf = 1 - zh
    ft_z = feat(zf, 0)

    def add_block(side, f, first=False):
        at = pl.ds(pl.multiple_of(f * width, 64), width)
        term = matmul(emb[f, side], projs[side][at, :], (0, 0))
        z[side] = term if first else z[side] + term

    def emb_gather(side, where):
        def block(k, part_=None):
            f = feat((zf, zh)[where], k)
            return emb.at[f, side] if part_ is None else emb.at[f, side, pl.ds(part_ * mid, mid)]

        return Gather(post, slot("emb_x", (side * 2 + where) * 4), x_peer, block)

    def emb_send_z(side):
        own = emb.at[ft, side]
        return post(own, own, slot("emb_z", side), z_peer)

    def emb_relay(g, side, zz):
        g.relay_left()
        g.relay_right()
        add_block(side, feat(zz, 3))
        add_block(side, feat(zz, 1))

    stats = {}

    def stat_a(k, value):
        n = value.shape[0]
        a = st_a.at[k, me_p, pl.ds(0, n)]
        a[...] = value
        stats[k, 0] = n, [
            post(a, a, slot("st_a", k * 7 + j), yc_peer(*to)) for j, to in enumerate(yc)]

    def stat_b(k):
        n, copies = stats[k, 0]
        for copy in copies:
            copy.wait_recv()
        b = st_b.at[k, zl, pl.ds(0, n)]
        b[...] = jnp.sum(st_a[k, :, :n], axis=0)
        stats[k, 1] = [
            post(b, b, slot("st_b", k * 3 + i - 1), zl_peer(i)) for i in (1, 2, 3)]

    def stat_c(k):
        for copy in stats[k, 1]:
            copy.wait_recv()
        return jnp.sum(st_b[k, :, :stats[k, 0][0]], axis=0)

    def forward_stats(side):
        v = z[side]
        stat_a(side, jnp.concatenate([fold(column(v)), fold(column(v * v))], axis=0))

    lanes = feats // LANES

    def forward_normalize(side):
        total = stat_c(side)
        center = unfold(total[:lanes]) / pairs
        spread = unfold(total[lanes:2 * lanes]) / pairs - center * center
        inv = lax.rsqrt(spread + EPS)
        z[side] = (z[side] - center) * inv
        return inv

    emb_zx = emb_send_z(TEXT)
    xn = emb_gather(TEXT, NEAR)
    xn.start()
    emb_zt = emb_send_z(TABLE)
    tn = emb_gather(TABLE, NEAR)
    tn.start()
    loads[3].wait()
    add_block(TEXT, ft, True)
    emb_relay(xn, TEXT, zh)
    emb_zx.wait_recv()
    xf = emb_gather(TEXT, FAR)
    xf.start()
    add_block(TEXT, ft_z)
    loads[2].wait()
    add_block(TABLE, ft, True)
    xn.finish()
    add_block(TEXT, feat(zh, 2))
    emb_relay(xf, TEXT, zf)
    emb_relay(tn, TABLE, zh)
    emb_zt.wait_recv()
    tf = emb_gather(TABLE, FAR)
    tf.start()
    add_block(TABLE, ft_z)
    xf.finish()
    add_block(TEXT, feat(zf, 2))
    forward_stats(TEXT)
    tn.finish()
    add_block(TABLE, feat(zh, 2))
    emb_relay(tf, TABLE, zf)
    stat_b(TEXT)
    tf.finish()
    add_block(TABLE, feat(zf, 2))
    forward_stats(TABLE)
    inv_text = forward_normalize(TEXT)

    half_full[ft] = z[TEXT].astype(BF16)

    def a2a(f, j):
        local = jnp.logical_and(f % 4 == y, f // 4 == c)
        copy = remote(
            half_full.at[f], txt_g.at[me_p], slot("txt_a2a", j),
            device(y_=f % 4, c_=f // 4), slot("txt_a2a") + me_p)

        @pl.when(jnp.logical_not(local))
        def _():
            copy.start()

        @pl.when(local)
        def _():
            txt_g[me_p] = half_full[f]

        def wait():
            @pl.when(jnp.logical_not(local))
            def _():
                copy.wait_send()

        drain.append(wait)

    def txt_gather(where):
        def block(k, part_=None):
            f = feat((zf, zh)[where], k)
            return half_full.at[f] if part_ is None else half_full.at[f, pl.ds(part_ * low, low)]

        return Gather(post, slot("txt_x", where * 4), x_peer, block)

    def tab_block(k, part_=None):
        p = ((y + k) % 4) * 2 + c
        return tab_g.at[p] if part_ is None else tab_g.at[p, pl.ds(part_ * low, low)]

    def tab_share(k):
        return post(tab_block(k), tab_block(k), slot("tab_c", k), c_peer)

    own = half_full.at[ft]
    txt_z = post(own, own, slot("txt_z"), z_peer)
    cn = txt_gather(NEAR)
    cn.start()
    a2a(ft, 0)
    stat_b(TABLE)
    cn.relay_left()
    a2a(feat(zh, 3), 1)
    cn.relay_right()
    a2a(feat(zh, 1), 2)
    inv_table = forward_normalize(TABLE)
    tab_g[me_p] = z[TABLE].astype(BF16)
    hn = Gather(post, slot("tab_y"), y_peer, tab_block)
    hn.start()
    shared = [tab_share(0)]
    txt_z.wait_recv()
    cf = txt_gather(FAR)
    cf.start()
    a2a(ft_z, 3)
    cn.finish()
    a2a(feat(zh, 2), 4)
    hn.relay_left()
    shared.append(tab_share(3))
    hn.relay_right()
    shared.append(tab_share(1))
    cf.relay_left()
    a2a(feat(zf, 3), 5)
    cf.relay_right()
    a2a(feat(zf, 1), 6)
    hn.finish()
    shared.append(tab_share(2))
    cf.finish()
    a2a(feat(zf, 2), 7)
    for copy in shared:
        copy.wait_recv()
    for j in range(1, 8):
        s = (me_p + j) % 8
        remote(txt_g.at[s], txt_g.at[s], slot("txt_a2a"), c_peer, slot("txt_a2a") + s).wait_recv()

    group = 8 * rows
    wide = feats // CHUNKS
    per_half = CHUNKS // 2
    at_l = pl.ds(pl.multiple_of((1 - l) * half, half), half)
    me_l = pl.ds(pl.multiple_of(l * half, half), half)
    chunks = [slice(k * wide, (k + 1) * wide) for k in range(CHUNKS)]
    halved = [slice(0, half), slice(half, feats)]
    row_index = ft * feats + lax.broadcasted_iota(jnp.int32, (feats, feats), 0)
    col_index = me_g * feats + lax.broadcasted_iota(jnp.int32, (feats, feats), 1)
    part[...] = matmul(tab_g[...].reshape(group, feats), txt_g[...].reshape(group, feats), (0, 0)) / pairs - (
        jnp.where(row_index == col_index, 0.25, 0.0))
    corr_l = []
    for k, cols in enumerate(chunks):
        part_s[k] = part[at_l, cols].astype(BF16)
        corr_l.append(post(part_s.at[k], part_r.at[k], slot("corr_l", k), l_peer))
    sums = halves.at[zl]
    sums[...] = jnp.concatenate(
        [fold(column(jnp.sum(g[...].astype(F32), axis=0))) for g in (tab_g, txt_g)], axis=0)
    half_sum = [post(sums, sums, slot("half_sum", i - 1), zl_peer(i)) for i in (1, 2, 3)]
    corr_h = []
    for k, cols in enumerate(chunks):
        corr_l[k].wait_recv()
        less = part[me_l, cols] + part_r[k].astype(F32)
        part_h[k] = less.astype(BF16)
        part[me_l, cols] = less
        corr_h.append(post(part_h.at[k], part_hr.at[k], slot("corr_h", k), h_peer))

    for copy in half_sum:
        copy.wait_recv()
    total = jnp.sum(halves[...], axis=0) / pairs
    mean_tab, mean_txt = unfold(total[:lanes]), unfold(total[lanes:])
    mean_tab = jnp.where(l == 0, mean_tab[:, :half], mean_tab[:, half:])
    loss_part, tab_back, txt_back = None, None, []
    ones = jnp.ones((16, wide), BF16)
    tab_rows = rows_of(mean_tab)
    for k, cols in enumerate(chunks):
        corr_h[k].wait_recv()
        less = part[me_l, cols] + part_hr[k].astype(F32)
        row_index = ft * feats + l * half + lax.broadcasted_iota(jnp.int32, (half, wide), 0)
        col_index = me_g * feats + k * wide + lax.broadcasted_iota(jnp.int32, (half, wide), 1)
        on_diag = row_index == col_index
        weighed = jnp.where(on_diag, less, OFF_WEIGHT * less)
        rounded = weighed.astype(BF16)
        ker[k, me_l, :] = rounded
        mine = ker.at[k, me_l]
        ker_l = post(mine, mine, slot("ker_l", k), l_peer)
        loss_k = column(0.5 * weighed * less)
        loss_part = loss_k if loss_part is None else loss_part + loss_k
        tilts = rounded.astype(F32) * jnp.where(on_diag, less + 1.0, less)
        high, rest = split(tilts)
        of_table = jnp.concatenate(
            [(matmul(ones, high, (1, 1)) + matmul(ones, rest, (1, 1)))[:1],
             column(matmul(rows_of(mean_txt[:, cols]), rounded, (1, 1)))], axis=0)
        tab_back = of_table if tab_back is None else tab_back + of_table
        txt_back.append((column(tilts), column(matmul(tab_rows, rounded, (1, 0)))))
        ker_l.wait_recv()
        hf, at = k // per_half, slice((k % per_half) * wide, (k % per_half + 1) * wide)
        dxp[hf, :, :, at] = matmul(tab_g[...].reshape(group, feats), ker[k], (1, 0)).astype(
            BF16).reshape(8, rows, wide)
        for j, (dy, dc) in enumerate(yc):
            post(dxp.at[hf, ((y + dy) % 4) * 2 + (c + dc) % 2, :, at], dx.at[hf, me_g, :, at],
                 slot("dx_a2a", k * 8 + j), yc_peer(dy, dc), slot("dx_a2a") + k * 8 + me_g)
        dx[hf, me_g, :, at] = dxp[hf, me_p, :, at]
    loss_row = column(fold(loss_part))
    value = jnp.concatenate(
        [fold(tab_back[:1]), fold(tab_back[1:]), loss_row, jnp.zeros((3, LANES), F32)], axis=0)
    mine = bt_a.at[me_p]
    mine[...] = value
    bt_a_copies = [post(mine, mine, slot("bt_a", j), yc_peer(*to)) for j, to in enumerate(yc)]
    bx_l[l] = jnp.concatenate([fold(t[i]) for i in (0, 1) for t in txt_back], axis=0)
    bx_l_copy = post(bx_l.at[l], bx_l.at[l], slot("bx_l"), l_peer)

    def dx_wait(k, g):
        @pl.when(g != me_g)
        def _():
            for q in range(per_half):
                ref = dx.at[k, g, :, q * wide:(q + 1) * wide]
                remote(ref, ref, slot("dx_a2a"), z_peer,
                       slot("dx_a2a") + (k * per_half + q) * 8 + g).wait_recv()

    txts = txt_g[...].reshape(group, feats)
    both = matmul(txts, jnp.concatenate([ker[k] for k in range(CHUNKS)], axis=1), (1, 1)).reshape(
        4, 2, rows, feats)
    for k in (0, 1):
        dtp[k] = both[:, k]
    dt_c = post(dtp.at[1 - c], dt_cr, slot("dt_c"), c_peer)

    def dt_src(k, part_):
        return dt_half.at[(y + k) % 4, pl.ds(part_ * low, low)]

    def dt_val(k, part_):
        return dt_cr[(y + k) % 4, part_ * low:(part_ + 1) * low, :]

    dt = Reduce(post, slot("dt_y"), y_peer, dt_src, dt_val, dt_buf)

    def dt_start():
        dt_c.wait_recv()
        for k in (2, 3, 1, 0):
            at = (y + k) % 4
            total = dtp[c, at] + dt_cr[at]
            dt_cr[at] = total
            dt_half[at] = total.astype(BF16)
            if k == 2:
                dt.send_opposite(0)
                dt.send_opposite(1)
            elif k:
                dt.send_direct(0 if k == 3 else 1)

    def dx_reduce(where):
        def src(k, part_):
            return dx.at[part_, feat((zf, zh)[where], k)]

        return Reduce(post, slot("dx_x", where * 6), x_peer, src,
                      lambda k, part_: src(k, part_)[...].astype(F32), dx_buf.at[where])

    dxr = [dx_reduce(FAR), dx_reduce(NEAR)]
    for k in (0, 1):
        if k == 1:
            dt_start()
            for copy in bt_a_copies:
                copy.wait_recv()
            bt_b[zl] = jnp.sum(bt_a[...], axis=0)
            bt_b_copies = [
                post(bt_b.at[zl], bt_b.at[zl], slot("bt_b", i - 1), zl_peer(i)) for i in (1, 2, 3)]
            bx_l_copy.wait_recv()
            bx_x[x] = bx_l[0] + bx_l[1]
            bx_x_copies = [post(bx_x.at[x], bx_x.at[x], slot("bx_x", i - 1), x_peer(i)) for i in (1, 2, 3)]
        for r, zz in zip(dxr, (zf, zh)):
            dx_wait(k, feat(zz, 2))
            r.send_opposite(k)
            dx_wait(k, feat(zz, (3, 1)[k]))
            r.send_direct(k)
        for r, zz in zip(dxr, (zf, zh)):
            dx_wait(k, feat(zz, (1, 3)[k]))
            r.pass_on(k)
            dx_wait(k, feat(zz, 0))
    for copy in bx_x_copies:
        copy.wait_recv()
    bx_z[zh] = jnp.sum(bx_x[...], axis=0)
    bx_z_copy = post(bx_z.at[zh], bx_z.at[zh], slot("bx_z"), z_peer)
    dt.pass_on(0)
    dt.pass_on(1)
    dx_z = []
    for k in (0, 1):
        dx_far[k] = dxr[FAR].total(k).astype(BF16)
        dx_z.append(post(dx_far.at[k], dx_zr.at[k], slot("dx_z", k), z_peer))
    for k in (0, 1):
        d[TABLE, pl.ds(k * low, low)] = dt.total(k)

    for copy in bt_b_copies:
        copy.wait_recv()
    pair = [bt_b[h * 2], bt_b[h * 2 + 1]]
    tilt_table, mean_table = [
        jnp.concatenate([unfold(v[i:i + 2]) for v in pair], axis=1) for i in (0, 2)]

    def backward(side, inv, mean, tilt):
        return (inv * (d[side] - mean - z[side] * tilt)).astype(BF16)

    loss_rows = jnp.sum(bt_b[...], axis=0)[4:5]
    ls_x[x] = jnp.broadcast_to(jnp.sum(loss_rows, axis=1, keepdims=True), (8, LANES))
    ls_copies = [post(ls_x.at[x], ls_x.at[x], slot("loss_x", i - 1), x_peer(i)) for i in (1, 2, 3)]

    def grad_reduce(side, where):
        def src(k, part_):
            return gp.at[side, where, k, pl.ds(part_ * mid, mid)]

        def val(k, part_):
            return g_own[side, where, k, part_ * mid:(part_ + 1) * mid, :]

        return Reduce(post, slot("gr_x", (side * 2 + where) * 6), x_peer, src, val,
                      gr_buf.at[side, where])

    def grad_terms(side, where, back, r):
        for k in (2, 3, 1, 0):
            at = pl.ds(pl.multiple_of(feat((zf, zh)[where], k) * width, 64), width)
            term = matmul(projs[side][at, :], back, (1, 1))
            if k:
                gp[side, where, k] = term.astype(BF16)
            if k != 2:
                g_own[side, where, k] = term
            if k == 2:
                r.send_opposite(0)
                r.send_opposite(1)
            elif k:
                r.send_direct(0 if k == 3 else 1)

    gr = [[grad_reduce(s, w) for w in (FAR, NEAR)] for s in (TABLE, TEXT)]
    grad_z = [None, None]

    def grad_far(side):
        for k in (0, 1):
            g_far[side, pl.ds(k * mid, mid)] = gr[side][FAR].total(k).astype(BF16)
        grad_z[side] = post(g_far.at[side], g_zr.at[side], slot("gr_z", side), z_peer)

    def grad_pass(side, where):
        gr[side][where].pass_on(0)
        gr[side][where].pass_on(1)

    back_table = backward(TABLE, inv_table, mean_table, tilt_table)
    grad_terms(TABLE, FAR, back_table, gr[TABLE][FAR])
    bx_z_copy.wait_recv()
    bx_y[me_p] = bx_z[0] + bx_z[1]
    bx_y_copies = [post(bx_y.at[me_p], bx_y.at[me_p], slot("bx_y", j), yc_peer(*to)) for j, to in enumerate(yc)]
    grad_terms(TABLE, NEAR, back_table, gr[TABLE][NEAR])
    for k, cols in enumerate(halved):
        v = dxr[NEAR].total(k)
        dx_z[k].wait_recv()
        d[TEXT, :, cols] = v + dx_zr[k].astype(F32)
    grad_pass(TABLE, FAR)
    for copy in bx_y_copies:
        copy.wait_recv()
    total = bx_y[(ft % 4) * 2 + ft // 4]
    tilt_text, mean_text = unfold(total[:lanes]), unfold(total[lanes:])
    back_text = backward(TEXT, inv_text, mean_text, tilt_text)
    grad_terms(TEXT, FAR, back_text, gr[TEXT][FAR])
    grad_far(TABLE)
    grad_pass(TABLE, NEAR)
    grad_terms(TEXT, NEAR, back_text, gr[TEXT][NEAR])
    grad_pass(TEXT, FAR)
    for copy in ls_copies:
        copy.wait_recv()
    ls_z[zh] = jnp.sum(ls_x[...], axis=0)
    ls_copy = post(ls_z.at[zh], ls_z.at[zh], slot("loss_z"), z_peer)
    grad_far(TEXT)
    grad_pass(TEXT, NEAR)

    def grad_near(side, out):
        near = [gr[side][NEAR].total(k) for k in (0, 1)]
        grad_z[side].wait_recv()
        for k in (0, 1):
            at = slice(k * mid, (k + 1) * mid)
            out[at, :] = near[k] + g_zr[side, at, :].astype(F32)

    grad_near(TABLE, grad_table)
    ls_copy.wait_recv()
    loss_out[...] = ((ls_z[0] + ls_z[1]) / (feats * NUM_FEAT))[:1, :1]
    grad_near(TEXT, grad_text)
    for wait in drain:
        wait()


def hand_kernel(a, b, oa, ob):
    oa[...] = a[...]
    ob[...] = b[...]


def hand_over(a, b):
    vmem = pl.BlockSpec(memory_space=pltpu.VMEM)
    return pl.pallas_call(
        hand_kernel,
        out_shape=(jax.ShapeDtypeStruct(a.shape, a.dtype), jax.ShapeDtypeStruct(b.shape, b.dtype)),
        in_specs=[vmem, vmem], out_specs=(vmem, vmem),
        name="hand_over",
    )(a, b)


def body(table, text, table_proj, text_proj):
    rows, width = table.shape
    depth, feats = table_proj.shape
    half, low = feats // 2, rows // 2
    vmem = pl.BlockSpec(memory_space=pltpu.VMEM)
    hbm = pl.BlockSpec(memory_space=pl.ANY)
    v = pltpu.VMEM
    grad_table, grad_text, loss = pl.pallas_call(
        kernel,
        out_shape=(
            jax.ShapeDtypeStruct((width, rows), F32),
            jax.ShapeDtypeStruct((width, rows), F32),
            jax.ShapeDtypeStruct((1, 1), F32),
        ),
        in_specs=[hbm, hbm, hbm, hbm],
        out_specs=(vmem, vmem, vmem),
        scratch_shapes=[
            v((depth, feats), BF16), v((depth, feats), BF16),
            v((NUM_FEAT, 2, width, rows), BF16),
            v((2, rows, feats), F32),
            v((2, 8, 8, LANES), F32), v((2, 4, 8, LANES), F32),
            v((NUM_FEAT, rows, feats), BF16),
            v((8, rows, feats), BF16), v((8, rows, feats), BF16),
            v((feats, feats), F32),
            v((CHUNKS, half, feats // CHUNKS), BF16), v((CHUNKS, half, feats // CHUNKS), BF16),
            v((CHUNKS, half, feats // CHUNKS), BF16), v((CHUNKS, half, feats // CHUNKS), BF16),
            v((CHUNKS, feats, feats // CHUNKS), BF16),
            v((2, 8, rows, half), BF16), v((2, 8, rows, half), BF16),
            v((2, 4, 2, rows, half), BF16),
            v((2, rows, half), BF16), v((2, rows, half), BF16),
            v((2, 4, rows, feats), F32), v((4, rows, feats), F32),
            v((4, rows, feats), BF16), v((4, 2, low, feats), BF16),
            v((2, rows, feats), F32),
            v((2, 2, 4, width, rows), BF16), v((2, 2, 4, width, rows), F32),
            v((2, 2, 4, 2, width // 2, rows), BF16),
            v((2, width, rows), BF16), v((2, width, rows), BF16),
            v((4, 8, LANES), F32), v((2, 8, LANES), F32),
            v((4, 8, LANES), F32),
            v((8, 8, LANES), F32), v((4, 8, LANES), F32),
            v((2, 8, LANES), F32), v((4, 8, LANES), F32),
            v((2, 8, LANES), F32), v((8, 8, LANES), F32),
            pltpu.SemaphoreType.DMA((NUM_SLOTS,)),
            pltpu.SemaphoreType.DMA((NUM_SLOTS,)),
            pltpu.SemaphoreType.DMA((4,)),
        ],
        compiler_params=pltpu.CompilerParams(
            collective_id=0, has_side_effects=True, vmem_limit_bytes=56 * 1024 * 1024
        ),
        cost_estimate=pl.CostEstimate(flops=3_500_000_000, bytes_accessed=9_000_000, transcendentals=2048),
        name="barlow_step",
    )(table.T, text.T, table_proj, text_proj)
    grad_table, grad_text = hand_over(grad_table, grad_text)
    return (grad_table.T, grad_text.T, loss.reshape(1))


def solution(mesh):
    placed = (P("dp", "feat"), P("dp", "feat"), P(None, "feat"), P(None, "feat"))
    return jax.shard_map(
        body,
        mesh=mesh,
        in_specs=placed,
        out_specs=(P("dp", "feat"), P("dp", "feat"), P()),
        check_vma=False,
    )
```
